32 devices in a mesh: ex: 8 (over z, y), hg: 4 (over x, core).
Axes of the slice: x: 2, y: 2, z: 4, core: 2. Of those that a mesh axis runs over, the one named last changes fastest.
Arguments:
- residual_in: bfloat16 [64, 2048], P('ex'), may hold values from -3 to 3
- queries: bfloat16 [64, 16, 576], P('ex', 'hg'), may hold values from -6 to 6
- new_latent: bfloat16 [64, 576], P('ex'), may hold values from -4 to 4
- cache: bfloat16 [64, 240, 576], P('ex'), may hold values from -4 to 4
- lengths: int32 [64], P('ex'), may hold values from 2 to 240, as said below
- value_up: bfloat16 [16, 512, 128], P('hg'), may hold values from -0.25 to 0.25
- out_proj: bfloat16 [16, 128, 2048], P('hg'), may hold values from -0.125 to 0.125
- norm_gain: float32 [2048], replicated, may hold values from 0.1 to 1.9
- routes: int32 [64, 6], P('ex'), may hold values from 0 to 63, as said below
- gate_weights: float32 [64, 6], P('ex'), may hold values from 0.05 to 0.6
- expert_gate_up: bfloat16 [64, 2, 1408, 2048], P('ex', None, 'hg'), may hold values from -0.125 to 0.125
- expert_down: bfloat16 [64, 1408, 2048], P('ex', 'hg'), may hold values from -0.15625 to 0.15625
- shared_gate_up: bfloat16 [2, 1408, 2048], P(None, 'hg'), may hold values from -0.125 to 0.125
- shared_down: bfloat16 [1408, 2048], P('hg'), may hold values from -0.15625 to 0.15625
Outputs:
- attended: bfloat16 [64, 2048], P('ex', 'hg')
- layer_out: bfloat16 [64, 2048], P('ex', 'hg')
The draws below stay inside these ranges and needn't reach their ends.
Inputs may be any that keep to these rules, and one draw needn't show every extreme that they name: `lengths`: some row has exactly 240 cached tokens. `routes`: each row names 6 different experts; the 8 rows of one device (aligned blocks of rows) name any one expert at most 2 times.
All inputs are finite; a program needn't handle non-finite values.
Results may differ from the reference program's by a relative error of at most 0.009.
Values may be sent and summed in bfloat16 or wider, within the bound.
A program may use at most 128 MiB of HBM per device.

```python
import math
import jax
import jax.numpy as jnp
from jax import lax

D = 2048
HEADS = 16
LATENT = 512
ROPE = 64
QK_NOPE = 128
HEAD_V = 128
EXPERTS = 64
TOP = 6
FF_E = 1408
SHARED_FF = 1408
CAP = 2
ROW_DEV = 8
CACHE = 240
ROWS = 64
KEYW = 576
N_EX = 8


def draw_residual_in(key, part):
    key = jax.random.fold_in(key, 3)
    column = jnp.arange(D).astype(jnp.float32)
    column_ramp = jnp.sqrt(1.0 + 4.0 * column / D)
    values = jnp.clip(0.35 * jax.random.normal(key, (ROWS, D), jnp.float32) * column_ramp, -3.0, 3.0)
    return values.astype(jnp.bfloat16)


def draw_queries(key, part):
    key = jax.random.fold_in(key, 1)
    key_base = jax.random.fold_in(key, 0)
    values = jnp.clip(1.5 * jax.random.normal(key_base, (ROWS, HEADS, KEYW), jnp.float32), -6.0, 6.0)
    return values.astype(jnp.bfloat16)


def draw_cache(key, part):
    key = jax.random.fold_in(key, 2)
    key_base = jax.random.fold_in(key, 0)
    values = jnp.clip(jax.random.normal(key_base, (ROWS, CACHE, KEYW), jnp.float32), -4.0, 4.0)
    return values.astype(jnp.bfloat16)


def draw_lengths(key, part):
    key = jax.random.fold_in(key, 4)
    key_lengths, key_full = jax.random.split(key, 2)
    drawn = jax.random.randint(key_lengths, (ROWS,), 2, CACHE + 1)
    full_row = jax.random.randint(key_full, (), 0, ROWS)
    return jnp.where(jnp.arange(ROWS) == full_row, CACHE, drawn).astype(jnp.int32)


def draw_routes(key, part):
    key = jax.random.fold_in(key, 5)
    blocks = ROWS // ROW_DEV
    half_picks = ROW_DEV * TOP // 2
    key_hot, key_count, key_blocks = jax.random.split(key, 3)
    hot_expert = jax.random.randint(key_hot, (), 0, EXPERTS)
    lowest = max(0, 2 * half_picks - 1 - EXPERTS)
    shared_count = jax.random.randint(key_count, (blocks,), lowest, half_picks)

    def one_block(block_key, count):
        key_perm, key_rows, key_cols = jax.random.split(block_key, 3)
        others = (hot_expert + 1 + jax.random.permutation(key_perm, EXPERTS - 1)) % EXPERTS
        place = jnp.arange(half_picks - 1)
        first_half = jnp.concatenate([hot_expert[None], others[place]])
        later = jnp.where(place < count, place, place + half_picks - 1 - count)
        second_half = jnp.concatenate([hot_expert[None], others[later]])
        table = jnp.concatenate([first_half, second_half]).reshape(ROW_DEV, TOP)
        table = table[jax.random.permutation(key_rows, ROW_DEV)]
        column_keys = jax.random.split(key_cols, ROW_DEV)
        column_order = jax.vmap(lambda single: jax.random.permutation(single, TOP))(column_keys)
        return jnp.take_along_axis(table, column_order, axis=1)
    block_keys = jax.random.split(key_blocks, blocks)
    return jax.vmap(one_block)(block_keys, shared_count).reshape(ROWS, TOP).astype(jnp.int32)


def block_levels(key, extent, cuts, low, high):
    level, own = 1.0, jax.random.fold_in(key, 6)
    for dim, parts in cuts:
        steps = jnp.exp(jax.random.uniform(jax.random.fold_in(own, dim), (parts,), jnp.float32, low / len(cuts), high / len(cuts)))
        level = level * jnp.repeat(steps, extent[dim] // parts).reshape([-1 if axis == dim else 1 for axis in range(len(extent))])
    return level


def gaussian(stream_key, dims, scale, most, cuts=(), kind=jnp.bfloat16):
    values = jax.random.normal(stream_key, dims, jnp.float32) * scale
    if len(cuts) > 0:
        values = block_levels(stream_key, dims, cuts, -0.22, 0.18) * values
    return jnp.clip(values, min=-most, max=most).astype(kind)


def setup_inputs(seed: int = 0) -> dict:
    splits = jax.random.split(jax.random.key(seed), 15)
    residual_in = draw_residual_in(jax.random.fold_in(splits[14], 71), 0)
    queries = draw_queries(jax.random.fold_in(splits[14], 71), 0)
    new_latent = gaussian(splits[2], (ROWS, KEYW), 1.0, 4.0, ((0, 8),))
    cache = draw_cache(jax.random.fold_in(splits[14], 71), 0)
    lengths = draw_lengths(jax.random.fold_in(splits[14], 71), 0)
    value_up = gaussian(splits[5], (HEADS, LATENT, HEAD_V), LATENT ** -0.5, 0.25, ((0, 4),))
    out_proj = gaussian(splits[6], (HEADS, HEAD_V, D), (HEADS * HEAD_V) ** -0.5, 0.125, ((0, 4),))
    norm_gain = jnp.clip(1.0 + 0.18 * jax.random.normal(splits[7], (D,), jnp.float32), 0.1, 1.9)
    routes = draw_routes(jax.random.fold_in(splits[14], 71), 0)
    gate_weights = jnp.clip(jnp.exp(math.log(0.6) - 2.4849067 * jax.random.uniform(splits[9], (ROWS, TOP), jnp.float32) ** block_levels(splits[9], (ROWS, TOP), ((0, 8),), -0.2, 0.2)), 0.05, 0.6)
    expert_gate_up = gaussian(splits[10], (EXPERTS, 2, FF_E, D), D ** -0.5, 0.125, ((0, 8), (2, 4)))
    expert_down = gaussian(splits[11], (EXPERTS, FF_E, D), FF_E ** -0.5, 0.15625, ((0, 8), (1, 4)))
    shared_gate_up = gaussian(splits[12], (2, SHARED_FF, D), D ** -0.5, 0.125, ((1, 4),))
    shared_down = gaussian(splits[13], (SHARED_FF, D), SHARED_FF ** -0.5, 0.15625, ((0, 4),))
    return dict(residual_in=residual_in, queries=queries, new_latent=new_latent, cache=cache, lengths=lengths, value_up=value_up, out_proj=out_proj, norm_gain=norm_gain, routes=routes, gate_weights=gate_weights, expert_gate_up=expert_gate_up, expert_down=expert_down, shared_gate_up=shared_gate_up, shared_down=shared_down)


norm_eps = 1e-06

def expert_outputs(normed, routes, expert_gate_up, expert_down):
    pairs = ROWS * TOP
    flat_routes = routes.reshape(pairs).astype(jnp.int32)
    sorted_pairs = jnp.argsort(flat_routes, stable=True).astype(jnp.int32)
    matches = (flat_routes[:, None] == jnp.arange(EXPERTS).astype(jnp.int32)[None, :]).astype(jnp.int32)
    counts = lax.optimization_barrier(jnp.sum(matches, axis=0)).astype(jnp.int32)
    starts = (jnp.cumsum(counts) - counts).astype(jnp.int32)
    slot_limit = CAP * N_EX

    def one_expert(expert):
        slot_ids = jnp.arange(slot_limit).astype(jnp.int32)
        is_live = slot_ids < counts[expert]
        position = jnp.clip(starts[expert] + slot_ids, 0, pairs - 1).astype(jnp.int32)
        pair_ids = jnp.where(is_live, sorted_pairs[position], pairs).astype(jnp.int32)
        row_data = normed[jnp.clip(pair_ids // TOP, 0, ROWS - 1).astype(jnp.int32)]
        gate_up = expert_gate_up[expert]
        gate_part = jnp.dot(row_data, gate_up[0].T, preferred_element_type=jnp.float32)
        up_part = jnp.dot(row_data, gate_up[1].T, preferred_element_type=jnp.float32)
        activation = (jax.nn.silu(gate_part) * up_part).astype(jnp.bfloat16)
        result = jnp.dot(activation, expert_down[expert], preferred_element_type=jnp.float32).astype(jnp.bfloat16)
        return (pair_ids, result)
    pair_ids, results = lax.map(one_expert, jnp.arange(EXPERTS).astype(jnp.int32))
    holder = jnp.zeros((pairs + 1, D), results.dtype)
    holder = holder.at[pair_ids.reshape(-1)].set(results.reshape(-1, D))
    return holder[:pairs].reshape(ROWS, TOP, D)

def reference(residual_in, queries, new_latent, cache, lengths, value_up, out_proj, norm_gain, routes, gate_weights, expert_gate_up, expert_down, shared_gate_up, shared_down):
    highest = lax.Precision.HIGHEST
    score_scale = (QK_NOPE + ROPE) ** (-0.5)
    query_f = queries.astype(jnp.float32)
    cache_f = cache.astype(jnp.float32)
    fresh_f = new_latent.astype(jnp.float32)
    scores = jnp.einsum('rhk,rtk->rht', query_f, cache_f, precision=highest) * score_scale
    own_score = jnp.einsum('rhk,rk->rh', query_f, fresh_f, precision=highest) * score_scale
    usable = jnp.arange(CACHE).astype(jnp.int32)[None, None, :] < lengths.astype(jnp.int32)[:, None, None]
    scores = jnp.where(usable, scores, -jnp.inf)
    peak = jnp.maximum(lax.optimization_barrier(jnp.max(scores, axis=2)), own_score)
    weights_cache = jnp.where(usable, jnp.exp(scores - peak[:, :, None]), 0.0)
    weight_own = jnp.exp(own_score - peak)
    denominator = lax.optimization_barrier(jnp.sum(weights_cache, axis=2)) + weight_own
    weights_bf = (weights_cache / denominator[:, :, None]).astype(jnp.bfloat16)
    own_bf = (weight_own / denominator).astype(jnp.bfloat16)
    latent_mix = jnp.einsum('rht,rtl->rhl', weights_bf.astype(jnp.float32), cache_f[:, :, :LATENT], precision=highest)
    latent_mix = latent_mix + own_bf.astype(jnp.float32)[:, :, None] * fresh_f[:, None, :LATENT]
    latent_mix = latent_mix.astype(jnp.bfloat16)
    head_out = jnp.einsum('rhl,hlv->rhv', latent_mix.astype(jnp.float32), value_up.astype(jnp.float32), precision=highest).astype(jnp.bfloat16)
    attention = jnp.einsum('rhv,hvd->rd', head_out.astype(jnp.float32), out_proj.astype(jnp.float32), precision=highest)
    hidden_state = residual_in.astype(jnp.float32) + attention
    attended = hidden_state.astype(jnp.bfloat16)
    inverse = lax.rsqrt(lax.optimization_barrier(jnp.mean(hidden_state * hidden_state, axis=1)) + norm_eps)
    normed = (hidden_state * inverse[:, None] * norm_gain).astype(jnp.bfloat16)
    expert_out = expert_outputs(normed, routes, expert_gate_up, expert_down)
    expert_f = lax.optimization_barrier(expert_out).astype(jnp.float32)
    shared_gate = jnp.dot(normed, shared_gate_up[0].T, preferred_element_type=jnp.float32)
    shared_up = jnp.dot(normed, shared_gate_up[1].T, preferred_element_type=jnp.float32)
    shared_act = (jax.nn.silu(shared_gate) * shared_up).astype(jnp.bfloat16)
    shared_out = jnp.dot(shared_act, shared_down, preferred_element_type=jnp.float32)
    weighted = lax.optimization_barrier(jnp.sum(gate_weights[:, :, None] * expert_f, axis=1))
    layer_out = (hidden_state + shared_out + weighted).astype(jnp.bfloat16)
    return (attended, layer_out)
```

```python
import functools

import jax
import jax.numpy as jnp
from jax import lax
from jax.experimental import pallas as pl
from jax.experimental.pallas import tpu as pltpu
from jax.sharding import PartitionSpec as P

LATENT = 512
ROPE = 64
QK_NOPE = 128
EXPERTS = 64
LANES = 128
TILE = 16
MESH = pl.DeviceIdType.MESH

norm_eps = 1e-06


def dot_nt(left, right):
    return lax.dot_general(left, right, (((1,), (1,)), ((), ())), preferred_element_type=jnp.float32)


def dot_nn(left, right):
    return jnp.dot(left, right, preferred_element_type=jnp.float32)


def kernel(
    n_ex,
    n_hg,
    lengths,
    residual,
    queries,
    new_latent,
    gain,
    routes,
    gates,
    cache,
    value_up,
    out_proj,
    gate_up,
    down,
    shared_gate_up,
    shared_down,
    attended_out,
    layer_out,
    kv,
    vu,
    op,
    gu,
    dn,
    sgu,
    sdn,
    mixes,
    attn_part,
    attn_got,
    gate_all,
    x_all,
    x_rows,
    act,
    sact,
    mine,
    part_send,
    part_got,
    row_part,
    row_got,
    hidden,
    kv_sem,
    vu_sem,
    op_sem,
    gu_sem,
    dn_sem,
    sh_sem,
    send_a,
    recv_a,
    send_g,
    recv_g,
    send_x,
    recv_x,
    send_h,
    recv_h,
    send_p,
    recv_p,
    send_r,
    recv_r,
):
    ex = lax.axis_index("ex")
    hg = lax.axis_index("hg")
    rows, slots, keyw = cache.shape
    heads = value_up.shape[0]
    local_experts, _, hidden_units, width = gate_up.shape
    quarter = width // n_hg
    half = quarter // 2
    all_rows = n_ex * rows
    piece = sgu.shape[1]
    pieces = -(-hidden_units // piece)

    kv_copies = [
        pltpu.make_async_copy(cache.at[r], kv.at[r, pl.ds(0, slots)], kv_sem.at[r])
        for r in range(rows)
    ]
    for copy in kv_copies:
        copy.start()
    vu_copy = pltpu.make_async_copy(value_up, vu, vu_sem)
    vu_copy.start()
    op_copy = pltpu.make_async_copy(out_proj, op, op_sem)
    op_copy.start()
    turn = lax.rem(ex, pieces)
    first = pl.multiple_of(
        piece * turn - (pieces * piece - hidden_units) * (turn // max(pieces - 1, 1)), TILE
    )
    sh_copies = [
        pltpu.make_async_copy(shared_gate_up.at[:, pl.ds(first, piece)], sgu, sh_sem.at[0]),
        pltpu.make_async_copy(shared_down.at[pl.ds(first, piece)], sdn, sh_sem.at[1]),
    ]
    for copy in sh_copies:
        copy.start()
    gu_copies = [
        pltpu.make_async_copy(gate_up.at[e], gu.at[e], gu_sem.at[e]) for e in range(local_experts)
    ]
    dn_copies = [
        pltpu.make_async_copy(down.at[e], dn.at[e], dn_sem.at[e]) for e in range(local_experts)
    ]
    for copy in gu_copies + dn_copies:
        copy.start()

    ex_peers = [lax.rem(ex + d, n_ex) for d in range(1, n_ex)]
    hg_peers = [lax.rem(hg + d, n_hg) for d in range(1, n_hg)]
    barrier = pltpu.get_barrier_semaphore()
    for peer in ex_peers:
        pl.semaphore_signal(barrier, inc=1, device_id=(peer, hg), device_id_type=MESH)
    for peer in hg_peers:
        pl.semaphore_signal(barrier, inc=1, device_id=(ex, peer), device_id_type=MESH)

    lane = lax.broadcasted_iota(jnp.int32, (rows, LANES), 1)
    dense = jnp.zeros((rows, LANES), jnp.float32)
    chosen, weight = routes[...], gates[...]
    for k in range(chosen.shape[1]):
        dense += jnp.where(lane == chosen[:, k : k + 1], weight[:, k : k + 1], 0.0)
    gate_all[ex] = dense
    fresh = new_latent[...].astype(jnp.float32)
    top = lax.broadcasted_iota(jnp.int32, (TILE, keyw), 0) == 0
    for r in range(rows):
        kv[r, pl.ds(slots, TILE)] = jnp.where(top, fresh[r : r + 1], 0.0).astype(jnp.bfloat16)

    pl.semaphore_wait(barrier, n_ex - 1 + n_hg - 1)
    gate_copies = []
    for peer in ex_peers:
        copy = pltpu.make_async_remote_copy(
            src_ref=gate_all.at[ex],
            dst_ref=gate_all.at[ex],
            send_sem=send_g.at[peer],
            recv_sem=recv_g.at[ex],
            device_id=(peer, hg),
            device_id_type=MESH,
        )
        copy.start()
        gate_copies.append(copy)

    scale = (QK_NOPE + ROPE) ** (-0.5)
    place = lax.broadcasted_iota(jnp.int32, (heads, slots + TILE), 1)
    for r in range(rows):
        kv_copies[r].wait()
        scores = dot_nt(queries[r], kv[r]) * scale
        usable = (place < lengths[r]) | (place == slots)
        scores = jnp.where(usable, scores, -jnp.inf)
        peak = jnp.max(scores, axis=1, keepdims=True)
        weights = jnp.where(usable, jnp.exp(scores - peak), 0.0)
        probs = (weights / jnp.sum(weights, axis=1, keepdims=True)).astype(jnp.bfloat16)
        mixes[pl.ds(r * heads, heads)] = dot_nn(probs, kv[r, :, :LATENT])
    count = rows * heads
    to_row = lax.broadcasted_iota(jnp.int32, (count, count), 0)
    from_row = lax.broadcasted_iota(jnp.int32, (count, count), 1)
    order = (from_row == lax.rem(to_row, rows) * heads + to_row // rows).astype(jnp.float32)
    by_head = dot_nn(order.astype(jnp.bfloat16), mixes[...].astype(jnp.bfloat16))
    vu_copy.wait()
    head_out = jnp.concatenate(
        [
            dot_nn(by_head[h * rows : (h + 1) * rows].astype(jnp.bfloat16), vu[h])
            for h in range(heads)
        ],
        axis=1,
    ).astype(jnp.bfloat16)
    op_copy.wait()
    proj = op[...].reshape(heads * op.shape[1], width)
    for part in range(n_hg):
        attn_part[part] = dot_nn(head_out, proj[:, part * quarter : (part + 1) * quarter])
    attn_copies = []
    for peer in hg_peers:
        copy = pltpu.make_async_remote_copy(
            src_ref=attn_part.at[peer],
            dst_ref=attn_got.at[hg],
            send_sem=send_a.at[peer],
            recv_sem=recv_a.at[hg],
            device_id=(ex, peer),
            device_id_type=MESH,
        )
        copy.start()
        attn_copies.append(copy)

    def arrived(buffer, peer, sem):
        pltpu.make_async_copy(buffer.at[peer], buffer.at[peer], sem.at[peer]).wait()

    columns = pl.ds(pl.multiple_of(hg * quarter, LANES), quarter)
    state = residual[:, columns].astype(jnp.float32) + attn_part[hg]
    for peer in hg_peers:
        arrived(attn_got, peer, recv_a)
        state += attn_got[peer]
    hidden[...] = state
    attended_out[...] = state.astype(jnp.bfloat16)
    squares = jnp.sum(state * state, axis=1, keepdims=True)
    high = squares.astype(jnp.bfloat16).astype(jnp.float32)
    scaled = state * gain[:, columns]
    packed = jnp.concatenate(
        [
            jnp.concatenate([scaled[:, :half], jnp.broadcast_to(high, (rows, LANES))], axis=1),
            jnp.concatenate(
                [scaled[:, half:], jnp.broadcast_to(squares - high, (rows, LANES))], axis=1
            ),
        ],
        axis=0,
    ).astype(jnp.bfloat16)
    x_all[hg, ex] = packed
    x_copies = []
    for peer in ex_peers:
        copy = pltpu.make_async_remote_copy(
            src_ref=x_all.at[hg, ex],
            dst_ref=x_all.at[hg, ex],
            send_sem=send_x.at[peer],
            recv_sem=recv_x.at[ex],
            device_id=(peer, hg),
            device_id_type=MESH,
        )
        copy.start()
        x_copies.append(copy)
    for peer in ex_peers:
        pltpu.make_async_copy(x_all.at[hg, peer], x_all.at[hg, peer], recv_x.at[peer]).wait()
    h_copies = []
    for peer in hg_peers:
        copy = pltpu.make_async_remote_copy(
            src_ref=x_all.at[hg],
            dst_ref=x_all.at[hg],
            send_sem=send_h.at[peer],
            recv_sem=recv_h.at[hg],
            device_id=(ex, peer),
            device_id_type=MESH,
        )
        copy.start()
        h_copies.append(copy)
    for peer in ex_peers:
        arrived(gate_all, peer, recv_g)
    for peer in hg_peers:
        arrived(x_all, peer, recv_h)

    total = jnp.zeros((all_rows, LANES), jnp.float32)
    for part in range(n_hg):
        block = x_all[part].astype(jnp.float32).reshape(n_ex, 2, rows, half + LANES)
        for side in range(2):
            flat = block[:, side].reshape(all_rows, half + LANES)
            start = part * quarter + side * half
            x_rows[:, start : start + half] = flat[:, :half].astype(jnp.bfloat16)
            total += flat[:, half:]
    inverse = lax.rsqrt(total[:, :1] / width + norm_eps)
    routed = gate_all[...].reshape(all_rows, LANES)
    lanes = lax.broadcasted_iota(jnp.int32, (all_rows, LANES), 1)

    def activate(gate_part, up_part, weight):
        gate_part = gate_part * inverse
        up_part = up_part * inverse
        return (gate_part / (1.0 + jnp.exp(-gate_part)) * up_part * weight).astype(jnp.bfloat16)

    for copy in sh_copies:
        copy.wait()
    unit = first + lax.broadcasted_iota(jnp.int32, (all_rows, piece), 1)
    sact[...] = activate(
        dot_nt(x_rows[...], sgu[0]),
        dot_nt(x_rows[...], sgu[1]),
        jnp.where(unit >= ex * piece, 1.0, 0.0),
    )

    def one_expert(e, carry):
        pltpu.make_async_copy(gate_up.at[e], gu.at[e], gu_sem.at[e]).wait()
        weight = jnp.sum(
            jnp.where(lanes == ex * local_experts + e, routed, 0.0), axis=1, keepdims=True
        )
        act[e] = activate(dot_nt(x_rows[...], gu[e, 0]), dot_nt(x_rows[...], gu[e, 1]), weight)
        return carry

    lax.fori_loop(0, local_experts, one_expert, 0)
    for copy in dn_copies:
        copy.wait()

    def down_part(part):
        where = pl.ds(pl.multiple_of(part * quarter, LANES), quarter)
        return lax.fori_loop(
            0,
            local_experts,
            lambda e, so_far: so_far + dot_nn(act[e], dn[e, :, where]),
            dot_nn(sact[...], sdn[:, where]),
            unroll=True,
        )

    p_copies = []
    for peer in hg_peers:
        part_send[peer] = down_part(peer).astype(jnp.bfloat16)
        copy = pltpu.make_async_remote_copy(
            src_ref=part_send.at[peer],
            dst_ref=part_got.at[hg],
            send_sem=send_p.at[peer],
            recv_sem=recv_p.at[hg],
            device_id=(ex, peer),
            device_id_type=MESH,
        )
        copy.start()
        p_copies.append(copy)
    mine[...] = down_part(hg)
    for peer in hg_peers:
        arrived(part_got, peer, recv_p)
    summed = mine[...]
    for peer in hg_peers:
        summed += part_got[peer].astype(jnp.float32)
    row_part[...] = summed.reshape(n_ex, rows, quarter)
    r_copies = []
    for peer in ex_peers:
        copy = pltpu.make_async_remote_copy(
            src_ref=row_part.at[peer],
            dst_ref=row_got.at[ex],
            send_sem=send_r.at[peer],
            recv_sem=recv_r.at[ex],
            device_id=(peer, hg),
            device_id_type=MESH,
        )
        copy.start()
        r_copies.append(copy)
    final = hidden[...] + row_part[ex]
    for peer in ex_peers:
        arrived(row_got, peer, recv_r)
        final += row_got[peer]
    layer_out[...] = final.astype(jnp.bfloat16)
    for copy in gate_copies + attn_copies + x_copies + h_copies + p_copies + r_copies:
        copy.wait_send()


def local(
    residual_in,
    queries,
    new_latent,
    cache,
    lengths,
    value_up,
    out_proj,
    norm_gain,
    routes,
    gate_weights,
    expert_gate_up,
    expert_down,
    shared_gate_up,
    shared_down,
):
    n_ex, n_hg = lax.axis_size("ex"), lax.axis_size("hg")
    rows, slots, keyw = cache.shape
    heads, _, head_v = value_up.shape
    local_experts, _, units, width = expert_gate_up.shape
    quarter = width // n_hg
    piece = -(-(units // TILE) // n_ex) * TILE
    bf16, f32 = jnp.bfloat16, jnp.float32
    vmem, dma = pltpu.VMEM, pltpu.SemaphoreType.DMA
    in_vmem, in_hbm = pl.BlockSpec(memory_space=pltpu.VMEM), pl.BlockSpec(memory_space=pl.ANY)
    out = jax.ShapeDtypeStruct((rows, quarter), bf16)
    return pl.pallas_call(
        functools.partial(kernel, n_ex, n_hg),
        out_shape=(out, out),
        in_specs=[pl.BlockSpec(memory_space=pltpu.SMEM)] + [in_vmem] * 6 + [in_hbm] * 7,
        out_specs=(in_vmem, in_vmem),
        scratch_shapes=[
            vmem((rows, slots + TILE, keyw), bf16),
            vmem(value_up.shape, bf16),
            vmem(out_proj.shape, bf16),
            vmem(expert_gate_up.shape, bf16),
            vmem(expert_down.shape, bf16),
            vmem((2, piece, width), bf16),
            vmem((piece, width), bf16),
            vmem((rows * heads, LATENT), f32),
            vmem((n_hg, rows, quarter), f32),
            vmem((n_hg, rows, quarter), f32),
            vmem((n_ex, rows, LANES), f32),
            vmem((n_hg, n_ex, 2 * rows, quarter // 2 + LANES), bf16),
            vmem((n_ex * rows, width), bf16),
            vmem((local_experts, n_ex * rows, units), bf16),
            vmem((n_ex * rows, piece), bf16),
            vmem((n_ex * rows, quarter), f32),
            vmem((n_hg, n_ex * rows, quarter), bf16),
            vmem((n_hg, n_ex * rows, quarter), bf16),
            vmem((n_ex, rows, quarter), f32),
            vmem((n_ex, rows, quarter), f32),
            vmem((rows, quarter), f32),
            dma((rows,)),
            dma,
            dma,
            dma((local_experts,)),
            dma((local_experts,)),
            dma((2,)),
            dma((n_hg,)),
            dma((n_hg,)),
            dma((n_ex,)),
            dma((n_ex,)),
            dma((n_ex,)),
            dma((n_ex,)),
            dma((n_hg,)),
            dma((n_hg,)),
            dma((n_hg,)),
            dma((n_hg,)),
            dma((n_ex,)),
            dma((n_ex,)),
        ],
        compiler_params=pltpu.CompilerParams(
            collective_id=0, has_side_effects=True, vmem_limit_bytes=58 * 1024 * 1024
        ),
    )(
        lengths,
        residual_in,
        queries,
        new_latent,
        norm_gain.reshape(1, -1),
        routes,
        gate_weights,
        cache,
        value_up,
        out_proj,
        expert_gate_up,
        expert_down,
        shared_gate_up,
        shared_down,
    )


def solution(mesh):
    placed = (
        P("ex", None),
        P("ex", "hg", None),
        P("ex", None),
        P("ex", None, None),
        P("ex"),
        P("hg", None, None),
        P("hg", None, None),
        P(),
        P("ex", None),
        P("ex", None),
        P("ex", None, "hg", None),
        P("ex", "hg", None),
        P(None, "hg", None),
        P("hg", None),
    )
    return jax.shard_map(
        local, mesh=mesh, in_specs=placed, out_specs=(P("ex", "hg"), P("ex", "hg")), check_vma=False
    )
```

```python
import functools

import jax
import jax.numpy as jnp
from jax import lax
from jax.experimental import pallas as pl
from jax.experimental.pallas import tpu as pltpu
from jax.sharding import PartitionSpec as P

LATENT = 512
ROPE = 64
QK_NOPE = 128
EXPERTS = 64
LANES = 128
TILE = 16
MESH = pl.DeviceIdType.MESH

norm_eps = 1e-06


def dot_nt(left, right):
    return lax.dot_general(left, right, (((1,), (1,)), ((), ())), preferred_element_type=jnp.float32)


def dot_nn(left, right):
    return jnp.dot(left, right, preferred_element_type=jnp.float32)


def kernel(
    n_ex,
    n_hg,
    lengths,
    residual,
    queries,
    new_latent,
    gain,
    routes,
    gates,
    cache,
    value_up,
    out_proj,
    gate_up,
    down,
    shared_gate_up,
    shared_down,
    outs,
    kv,
    vu,
    op,
    gu,
    dn,
    sgu,
    sdn,
    mixes,
    attn_part,
    attn_got,
    gate_all,
    x_all,
    x_rows,
    pairs,
    spairs,
    act,
    sact,
    mine,
    part_send,
    part_got,
    row_part,
    row_got,
    hidden,
    kv_sem,
    vu_sem,
    op_sem,
    gu_sem,
    dn_sem,
    sh_sem,
    send_a,
    recv_a,
    send_g,
    recv_g,
    send_x,
    recv_x,
    send_h,
    recv_h,
    send_p,
    recv_p,
    send_r,
    recv_r,
):
    ex = lax.axis_index("ex")
    hg = lax.axis_index("hg")
    rows, _, slots = cache.shape
    heads = value_up.shape[0]
    local_experts, _, hidden_units, width = gate_up.shape
    quarter = width // n_hg
    half = quarter // 2
    all_rows = n_ex * rows
    piece = sgu.shape[1]
    pieces = -(-hidden_units // piece)

    kv_copies = [
        pltpu.make_async_copy(cache.at[r], kv.at[r], kv_sem.at[r])
        for r in range(rows)
    ]
    for copy in kv_copies:
        copy.start()
    vu_copy = pltpu.make_async_copy(value_up, vu, vu_sem)
    vu_copy.start()
    op_copy = pltpu.make_async_copy(out_proj, op, op_sem)
    op_copy.start()
    turn = lax.rem(ex, pieces)
    first = pl.multiple_of(
        piece * turn - (pieces * piece - hidden_units) * (turn // max(pieces - 1, 1)), TILE
    )
    sh_copies = [
        pltpu.make_async_copy(shared_gate_up.at[:, pl.ds(first, piece)], sgu, sh_sem.at[0]),
        pltpu.make_async_copy(shared_down.at[pl.ds(first, piece)], sdn, sh_sem.at[1]),
    ]
    for copy in sh_copies:
        copy.start()
    gu_copies = [
        pltpu.make_async_copy(gate_up.at[e], gu.at[e], gu_sem.at[e]) for e in range(local_experts)
    ]
    dn_copies = [
        pltpu.make_async_copy(down.at[e], dn.at[e], dn_sem.at[e]) for e in range(local_experts)
    ]
    early = local_experts * 3 // 8
    for copy in gu_copies[:early]:
        copy.start()

    ex_peers = [lax.rem(ex + d, n_ex) for d in range(1, n_ex)]
    pair = 2 - n_hg % 2
    hg_peers = []
    for d in range(0, n_hg, pair):
        base = lax.rem(hg + d, n_hg)
        other = base + 1 - 2 * lax.rem(base, 2)
        hg_peers += ([base] if d else []) + ([other] if pair == 2 else [])
    barrier = pltpu.get_barrier_semaphore()
    for peer in ex_peers:
        pl.semaphore_signal(barrier, inc=1, device_id=(peer, hg), device_id_type=MESH)
    for peer in hg_peers:
        pl.semaphore_signal(barrier, inc=1, device_id=(ex, peer), device_id_type=MESH)

    lane = lax.broadcasted_iota(jnp.int32, (rows, LANES), 1)
    dense = jnp.zeros((rows, LANES), jnp.float32)
    chosen, weight = routes[...], gates[...]
    for k in range(chosen.shape[1]):
        dense += jnp.where(lane == chosen[:, k : k + 1], weight[:, k : k + 1], 0.0)
    gate_all[ex] = dense

    pl.semaphore_wait(barrier, n_ex - 1 + n_hg - 1)
    gate_copies = []
    for peer in ex_peers:
        copy = pltpu.make_async_remote_copy(
            src_ref=gate_all.at[ex],
            dst_ref=gate_all.at[ex],
            send_sem=send_g.at[peer],
            recv_sem=recv_g.at[ex],
            device_id=(peer, hg),
            device_id_type=MESH,
        )
        copy.start()
        gate_copies.append(copy)

    scale = (QK_NOPE + ROPE) ** (-0.5)
    fresh = new_latent[...].astype(jnp.float32)
    place = lax.broadcasted_iota(jnp.int32, (heads, slots), 1)
    for r in range(rows):
        own = (
            jnp.sum(queries[r].astype(jnp.float32) * fresh[r : r + 1], axis=1, keepdims=True)
            * scale
        )
        kv_copies[r].wait()
        usable = place < lengths[r]
        scores = jnp.where(usable, dot_nn(queries[r], kv[r]) * scale, -jnp.inf)
        peak = jnp.maximum(jnp.max(scores, axis=1, keepdims=True), own)
        weights = jnp.where(usable, jnp.exp(scores - peak), 0.0)
        weight_own = jnp.exp(own - peak)
        share = 1.0 / (jnp.sum(weights, axis=1, keepdims=True) + weight_own)
        probs = (weights * share).astype(jnp.bfloat16)
        probs_own = (weight_own * share).astype(jnp.bfloat16).astype(jnp.float32)
        mixes[pl.ds(r * heads, heads)] = (
            dot_nt(probs, kv[r, :LATENT]) + probs_own * fresh[r : r + 1, :LATENT]
        )
    count = rows * heads
    to_row = lax.broadcasted_iota(jnp.int32, (count, count), 0)
    from_row = lax.broadcasted_iota(jnp.int32, (count, count), 1)
    order = (from_row == lax.rem(to_row, rows) * heads + to_row // rows).astype(jnp.float32)
    by_head = dot_nn(order.astype(jnp.bfloat16), mixes[...].astype(jnp.bfloat16))
    vu_copy.wait()
    head_out = jnp.concatenate(
        [
            dot_nn(by_head[h * rows : (h + 1) * rows].astype(jnp.bfloat16), vu[h])
            for h in range(heads)
        ],
        axis=1,
    ).astype(jnp.bfloat16)
    op_copy.wait()
    proj = op[...].reshape(heads * op.shape[1], width)
    for part in range(n_hg):
        attn_part[part] = dot_nn(head_out, proj[:, part * quarter : (part + 1) * quarter])
    attn_copies = []
    for peer in hg_peers:
        copy = pltpu.make_async_remote_copy(
            src_ref=attn_part.at[peer],
            dst_ref=attn_got.at[hg],
            send_sem=send_a.at[peer],
            recv_sem=recv_a.at[hg],
            device_id=(ex, peer),
            device_id_type=MESH,
        )
        copy.start()
        attn_copies.append(copy)
    for copy in gu_copies[early:]:
        copy.start()

    def arrived(buffer, peer, sem):
        pltpu.make_async_copy(buffer.at[peer], buffer.at[peer], sem.at[peer]).wait()

    columns = pl.ds(pl.multiple_of(hg * quarter, LANES), quarter)
    state = residual[:, columns].astype(jnp.float32) + attn_part[hg]
    for peer in hg_peers:
        arrived(attn_got, peer, recv_a)
        state += attn_got[peer]
    hidden[...] = state
    outs[0] = state
    squares = jnp.sum(state * state, axis=1, keepdims=True)
    high = squares.astype(jnp.bfloat16).astype(jnp.float32)
    scaled = state * gain[:, columns]
    packed = jnp.concatenate(
        [
            jnp.concatenate([scaled[:, :half], jnp.broadcast_to(high, (rows, LANES))], axis=1),
            jnp.concatenate(
                [scaled[:, half:], jnp.broadcast_to(squares - high, (rows, LANES))], axis=1
            ),
        ],
        axis=0,
    ).astype(jnp.bfloat16)
    x_all[hg, ex] = packed
    x_copies = []
    for peer in ex_peers:
        copy = pltpu.make_async_remote_copy(
            src_ref=x_all.at[hg, ex],
            dst_ref=x_all.at[hg, ex],
            send_sem=send_x.at[peer],
            recv_sem=recv_x.at[ex],
            device_id=(peer, hg),
            device_id_type=MESH,
        )
        copy.start()
        x_copies.append(copy)
    for peer in ex_peers:
        pltpu.make_async_copy(x_all.at[hg, peer], x_all.at[hg, peer], recv_x.at[peer]).wait()
    h_copies = []
    for peer in hg_peers:
        copy = pltpu.make_async_remote_copy(
            src_ref=x_all.at[hg],
            dst_ref=x_all.at[hg],
            send_sem=send_h.at[peer],
            recv_sem=recv_h.at[hg],
            device_id=(ex, peer),
            device_id_type=MESH,
        )
        copy.start()
        h_copies.append(copy)
    for copy in dn_copies:
        copy.start()
    for peer in ex_peers:
        arrived(gate_all, peer, recv_g)

    for copy in sh_copies + gu_copies:
        copy.wait()
    total = jnp.zeros((all_rows, LANES), jnp.float32)
    for number, part in enumerate([hg] + hg_peers):
        if number:
            arrived(x_all, part, recv_h)
        block = x_all[part].astype(jnp.float32).reshape(n_ex, 2, rows, half + LANES)
        sides = [block[:, side].reshape(all_rows, half + LANES) for side in range(2)]
        x_rows[:, :half] = sides[0][:, :half].astype(jnp.bfloat16)
        x_rows[:, half:] = sides[1][:, :half].astype(jnp.bfloat16)
        total += sides[0][:, half:] + sides[1][:, half:]
        where = pl.ds(pl.multiple_of(part * quarter, LANES), quarter)
        values = x_rows[...]
        for j in range(2):
            product = dot_nt(values, sgu[j, :, where])
            spairs[j] = product if number == 0 else spairs[j] + product

        def one_expert(e, carry):
            for j in range(2):
                product = dot_nt(values, gu[e, j, :, where])
                pairs[e, j] = product if number == 0 else pairs[e, j] + product
            return carry

        lax.fori_loop(0, local_experts, one_expert, 0, unroll=True)
    inverse = lax.rsqrt(total[:, :1] / width + norm_eps)
    routed = gate_all[...].reshape(all_rows, LANES)
    lanes = lax.broadcasted_iota(jnp.int32, (all_rows, LANES), 1)

    def activate(gate_part, up_part, weight):
        gate_part = gate_part * inverse
        up_part = up_part * inverse
        return (gate_part / (1.0 + jnp.exp(-gate_part)) * up_part * weight).astype(jnp.bfloat16)

    unit = first + lax.broadcasted_iota(jnp.int32, (all_rows, piece), 1)
    sact[...] = activate(spairs[0], spairs[1], jnp.where(unit >= ex * piece, 1.0, 0.0))

    def finish_expert(e, carry):
        weight = jnp.sum(
            jnp.where(lanes == ex * local_experts + e, routed, 0.0), axis=1, keepdims=True
        )
        act[e] = activate(pairs[e, 0], pairs[e, 1], weight)
        return carry

    lax.fori_loop(0, local_experts, finish_expert, 0)
    for copy in dn_copies:
        copy.wait()

    def down_part(part):
        where = pl.ds(pl.multiple_of(part * quarter, LANES), quarter)
        return lax.fori_loop(
            0,
            local_experts,
            lambda e, so_far: so_far + dot_nn(act[e], dn[e, :, where]),
            dot_nn(sact[...], sdn[:, where]),
            unroll=True,
        )

    p_copies = []
    for peer in hg_peers:
        part_send[peer] = down_part(peer).astype(jnp.bfloat16)
        copy = pltpu.make_async_remote_copy(
            src_ref=part_send.at[peer],
            dst_ref=part_got.at[hg],
            send_sem=send_p.at[peer],
            recv_sem=recv_p.at[hg],
            device_id=(ex, peer),
            device_id_type=MESH,
        )
        copy.start()
        p_copies.append(copy)
    mine[...] = down_part(hg)
    for peer in hg_peers:
        arrived(part_got, peer, recv_p)
    summed = mine[...]
    for peer in hg_peers:
        summed += part_got[peer].astype(jnp.float32)
    row_part[...] = summed.reshape(n_ex, rows, quarter)
    r_copies = []
    for peer in ex_peers:
        copy = pltpu.make_async_remote_copy(
            src_ref=row_part.at[peer],
            dst_ref=row_got.at[ex],
            send_sem=send_r.at[peer],
            recv_sem=recv_r.at[ex],
            device_id=(peer, hg),
            device_id_type=MESH,
        )
        copy.start()
        r_copies.append(copy)
    final = hidden[...] + row_part[ex]
    for peer in ex_peers:
        arrived(row_got, peer, recv_r)
        final += row_got[peer]
    outs[1] = final
    for copy in gate_copies + attn_copies + x_copies + h_copies + p_copies + r_copies:
        copy.wait_send()


def local(
    residual_in,
    queries,
    new_latent,
    cache,
    lengths,
    value_up,
    out_proj,
    norm_gain,
    routes,
    gate_weights,
    expert_gate_up,
    expert_down,
    shared_gate_up,
    shared_down,
):
    n_ex, n_hg = lax.axis_size("ex"), lax.axis_size("hg")
    rows, slots, keyw = cache.shape
    heads, _, head_v = value_up.shape
    local_experts, _, units, width = expert_gate_up.shape
    quarter = width // n_hg
    piece = -(-(units // TILE) // n_ex) * TILE
    bf16, f32 = jnp.bfloat16, jnp.float32
    vmem, dma = pltpu.VMEM, pltpu.SemaphoreType.DMA
    in_vmem, in_hbm = pl.BlockSpec(memory_space=pltpu.VMEM), pl.BlockSpec(memory_space=pl.ANY)
    outs = pl.pallas_call(
        functools.partial(kernel, n_ex, n_hg),
        out_shape=jax.ShapeDtypeStruct((2, rows, quarter), f32),
        in_specs=[pl.BlockSpec(memory_space=pltpu.SMEM)] + [in_vmem] * 6 + [in_hbm] * 7,
        out_specs=in_vmem,
        scratch_shapes=[
            vmem((rows, keyw, slots), bf16),
            vmem(value_up.shape, bf16),
            vmem(out_proj.shape, bf16),
            vmem(expert_gate_up.shape, bf16),
            vmem(expert_down.shape, bf16),
            vmem((2, piece, width), bf16),
            vmem((piece, width), bf16),
            vmem((rows * heads, LATENT), f32),
            vmem((n_hg, rows, quarter), f32),
            vmem((n_hg, rows, quarter), f32),
            vmem((n_ex, rows, LANES), f32),
            vmem((n_hg, n_ex, 2 * rows, quarter // 2 + LANES), bf16),
            vmem((n_ex * rows, quarter), bf16),
            vmem((local_experts, 2, n_ex * rows, units), f32),
            vmem((2, n_ex * rows, piece), f32),
            vmem((local_experts, n_ex * rows, units), bf16),
            vmem((n_ex * rows, piece), bf16),
            vmem((n_ex * rows, quarter), f32),
            vmem((n_hg, n_ex * rows, quarter), bf16),
            vmem((n_hg, n_ex * rows, quarter), bf16),
            vmem((n_ex, rows, quarter), f32),
            vmem((n_ex, rows, quarter), f32),
            vmem((rows, quarter), f32),
            dma((rows,)),
            dma,
            dma,
            dma((local_experts,)),
            dma((local_experts,)),
            dma((2,)),
            dma((n_hg,)),
            dma((n_hg,)),
            dma((n_ex,)),
            dma((n_ex,)),
            dma((n_ex,)),
            dma((n_ex,)),
            dma((n_hg,)),
            dma((n_hg,)),
            dma((n_hg,)),
            dma((n_hg,)),
            dma((n_ex,)),
            dma((n_ex,)),
        ],
        compiler_params=pltpu.CompilerParams(
            collective_id=0, has_side_effects=True, vmem_limit_bytes=58 * 1024 * 1024
        ),
    )(
        lengths,
        residual_in,
        queries,
        new_latent,
        norm_gain.reshape(1, -1),
        routes,
        gate_weights,
        jnp.swapaxes(cache, 1, 2),
        value_up,
        out_proj,
        expert_gate_up,
        expert_down,
        shared_gate_up,
        shared_down,
    )
    return outs[0].astype(bf16), outs[1].astype(bf16)


def solution(mesh):
    placed = (
        P("ex", None),
        P("ex", "hg", None),
        P("ex", None),
        P("ex", None, None),
        P("ex"),
        P("hg", None, None),
        P("hg", None, None),
        P(),
        P("ex", None),
        P("ex", None),
        P("ex", None, "hg", None),
        P("ex", "hg", None),
        P(None, "hg", None),
        P("hg", None),
    )
    return jax.shard_map(
        local, mesh=mesh, in_specs=placed, out_specs=(P("ex", "hg"), P("ex", "hg")), check_vma=False
    )
```

```python
import functools

import jax
import jax.numpy as jnp
from jax import lax
from jax.experimental import pallas as pl
from jax.experimental.pallas import tpu as pltpu
from jax.sharding import PartitionSpec as P

LATENT = 512
ROPE = 64
QK_NOPE = 128
EXPERTS = 64
LANES = 128
TILE = 16
MESH = pl.DeviceIdType.MESH

norm_eps = 1e-06


def dot_nt(left, right):
    return lax.dot_general(left, right, (((1,), (1,)), ((), ())), preferred_element_type=jnp.float32)


def dot_nn(left, right):
    return jnp.dot(left, right, preferred_element_type=jnp.float32)


def kernel(
    n_ex,
    n_hg,
    lengths,
    residual,
    queries,
    new_latent,
    gain,
    routes,
    gates,
    cache,
    value_up,
    out_proj,
    gate_up,
    down,
    shared_gate_up,
    shared_down,
    outs,
    kv,
    vu,
    op,
    gu,
    dn,
    sgu,
    sdn,
    mixes,
    attn_part,
    attn_got,
    gate_all,
    x_all,
    x_rows,
    pairs,
    spairs,
    act,
    sact,
    mine,
    part_send,
    part_got,
    row_part,
    row_got,
    hidden,
    kv_sem,
    vu_sem,
    op_sem,
    gu_sem,
    dn_sem,
    sh_sem,
    send_a,
    recv_a,
    send_g,
    recv_g,
    send_x,
    recv_x,
    send_h,
    recv_h,
    send_p,
    recv_p,
    send_r,
    recv_r,
):
    ex = lax.axis_index("ex")
    hg = lax.axis_index("hg")
    rows, _, slots = cache.shape
    heads = value_up.shape[0]
    local_experts, _, hidden_units, width = gate_up.shape
    quarter = width // n_hg
    half = quarter // 2
    all_rows = n_ex * rows
    piece = sgu.shape[1]
    pieces = -(-hidden_units // piece)

    kv_copies = [
        pltpu.make_async_copy(cache.at[r], kv.at[r], kv_sem.at[r])
        for r in range(rows)
    ]
    for copy in kv_copies:
        copy.start()
    vu_copy = pltpu.make_async_copy(value_up, vu, vu_sem)
    vu_copy.start()
    op_copy = pltpu.make_async_copy(out_proj, op, op_sem)
    op_copy.start()
    turn = lax.rem(ex, pieces)
    first = pl.multiple_of(
        piece * turn - (pieces * piece - hidden_units) * (turn // max(pieces - 1, 1)), TILE
    )
    sh_copies = [
        pltpu.make_async_copy(shared_gate_up.at[:, pl.ds(first, piece)], sgu, sh_sem.at[0]),
        pltpu.make_async_copy(shared_down.at[pl.ds(first, piece)], sdn, sh_sem.at[1]),
    ]
    for copy in sh_copies:
        copy.start()
    gu_copies = [
        pltpu.make_async_copy(gate_up.at[e], gu.at[e], gu_sem.at[e]) for e in range(local_experts)
    ]
    dn_copies = [
        pltpu.make_async_copy(down.at[e], dn.at[e], dn_sem.at[e]) for e in range(local_experts)
    ]
    early = local_experts * 3 // 8
    for copy in gu_copies[:early]:
        copy.start()

    ex_peers = [lax.rem(ex + d, n_ex) for d in range(1, n_ex)]
    pair = 2 - n_hg % 2
    hg_peers = []
    for d in range(0, n_hg, pair):
        base = lax.rem(hg + d, n_hg)
        other = base + 1 - 2 * lax.rem(base, 2)
        hg_peers += ([base] if d else []) + ([other] if pair == 2 else [])
    barrier = pltpu.get_barrier_semaphore()
    for peer in ex_peers:
        pl.semaphore_signal(barrier, inc=1, device_id=(peer, hg), device_id_type=MESH)
    for peer in hg_peers:
        pl.semaphore_signal(barrier, inc=1, device_id=(ex, peer), device_id_type=MESH)

    lane = lax.broadcasted_iota(jnp.int32, (rows, LANES), 1)
    dense = jnp.zeros((rows, LANES), jnp.float32)
    chosen, weight = routes[...], gates[...]
    for k in range(chosen.shape[1]):
        dense += jnp.where(lane == chosen[:, k : k + 1], weight[:, k : k + 1], 0.0)
    gate_all[ex] = dense

    pl.semaphore_wait(barrier, n_ex - 1 + n_hg - 1)
    gate_copies = []
    for peer in ex_peers:
        copy = pltpu.make_async_remote_copy(
            src_ref=gate_all.at[ex],
            dst_ref=gate_all.at[ex],
            send_sem=send_g.at[peer],
            recv_sem=recv_g.at[ex],
            device_id=(peer, hg),
            device_id_type=MESH,
        )
        copy.start()
        gate_copies.append(copy)

    scale = (QK_NOPE + ROPE) ** (-0.5)
    fresh = new_latent[...].astype(jnp.float32)
    place = lax.broadcasted_iota(jnp.int32, (heads, slots), 1)
    for r in range(rows):
        own = (
            jnp.sum(queries[r].astype(jnp.float32) * fresh[r : r + 1], axis=1, keepdims=True)
            * scale
        )
        kv_copies[r].wait()
        usable = place < lengths[r]
        scores = jnp.where(usable, dot_nn(queries[r], kv[r]) * scale, -jnp.inf)
        peak = jnp.maximum(jnp.max(scores, axis=1, keepdims=True), own)
        weights = jnp.where(usable, jnp.exp(scores - peak), 0.0)
        weight_own = jnp.exp(own - peak)
        share = 1.0 / (jnp.sum(weights, axis=1, keepdims=True) + weight_own)
        probs = (weights * share).astype(jnp.bfloat16)
        probs_own = (weight_own * share).astype(jnp.bfloat16).astype(jnp.float32)
        mixes[pl.ds(r * heads, heads)] = (
            dot_nt(probs, kv[r, :LATENT]) + probs_own * fresh[r : r + 1, :LATENT]
        )
    count = rows * heads
    to_row = lax.broadcasted_iota(jnp.int32, (count, count), 0)
    from_row = lax.broadcasted_iota(jnp.int32, (count, count), 1)
    order = (from_row == lax.rem(to_row, rows) * heads + to_row // rows).astype(jnp.float32)
    by_head = dot_nn(order.astype(jnp.bfloat16), mixes[...].astype(jnp.bfloat16))
    vu_copy.wait()
    head_out = jnp.concatenate(
        [
            dot_nn(by_head[h * rows : (h + 1) * rows].astype(jnp.bfloat16), vu[h])
            for h in range(heads)
        ],
        axis=1,
    ).astype(jnp.bfloat16)
    op_copy.wait()

    def project(part):
        where = pl.ds(pl.multiple_of(part * quarter, LANES), quarter)
        attn_part[part] = dot_nn(head_out, op[:, :, where].reshape(heads * op.shape[1], quarter))

    attn_copies = []
    for peer in hg_peers[::-1]:
        project(peer)
        copy = pltpu.make_async_remote_copy(
            src_ref=attn_part.at[peer],
            dst_ref=attn_got.at[hg],
            send_sem=send_a.at[peer],
            recv_sem=recv_a.at[hg],
            device_id=(ex, peer),
            device_id_type=MESH,
        )
        copy.start()
        attn_copies.append(copy)
    project(hg)
    for copy in gu_copies[early:]:
        copy.start()

    def arrived(buffer, peer, sem):
        pltpu.make_async_copy(buffer.at[peer], buffer.at[peer], sem.at[peer]).wait()

    columns = pl.ds(pl.multiple_of(hg * quarter, LANES), quarter)
    state = residual[:, columns].astype(jnp.float32) + attn_part[hg]
    for peer in hg_peers:
        arrived(attn_got, peer, recv_a)
        state += attn_got[peer]
    hidden[...] = state
    outs[0] = state
    squares = jnp.sum(state * state, axis=1, keepdims=True)
    high = squares.astype(jnp.bfloat16).astype(jnp.float32)
    scaled = state * gain[:, columns]
    packed = jnp.concatenate(
        [
            jnp.concatenate([scaled[:, :half], jnp.broadcast_to(high, (rows, LANES))], axis=1),
            jnp.concatenate(
                [scaled[:, half:], jnp.broadcast_to(squares - high, (rows, LANES))], axis=1
            ),
        ],
        axis=0,
    ).astype(jnp.bfloat16)
    x_all[hg, ex] = packed
    x_copies = []
    for peer in ex_peers:
        copy = pltpu.make_async_remote_copy(
            src_ref=x_all.at[hg, ex],
            dst_ref=x_all.at[hg, ex],
            send_sem=send_x.at[peer],
            recv_sem=recv_x.at[ex],
            device_id=(peer, hg),
            device_id_type=MESH,
        )
        copy.start()
        x_copies.append(copy)
    for peer in ex_peers:
        pltpu.make_async_copy(x_all.at[hg, peer], x_all.at[hg, peer], recv_x.at[peer]).wait()
    h_copies = []

    def share(part, peer, slot):
        copy = pltpu.make_async_remote_copy(
            src_ref=x_all.at[part],
            dst_ref=x_all.at[part],
            send_sem=send_h.at[slot],
            recv_sem=recv_h.at[part],
            device_id=(ex, peer),
            device_id_type=MESH,
        )
        copy.start()
        h_copies.append(copy)

    relay = n_hg == 4
    for peer in (hg_peers[1::-1] if relay else hg_peers):
        share(hg, peer, peer)
    for copy in dn_copies:
        copy.start()
    for peer in ex_peers:
        arrived(gate_all, peer, recv_g)

    for copy in sh_copies + gu_copies:
        copy.wait()
    total = jnp.zeros((all_rows, LANES), jnp.float32)
    for number, part in enumerate([hg] + hg_peers):
        if number:
            arrived(x_all, part, recv_h)
        if relay and number == 2:
            share(part, hg_peers[0], hg_peers[2])
        block = x_all[part].astype(jnp.float32).reshape(n_ex, 2, rows, half + LANES)
        sides = [block[:, side].reshape(all_rows, half + LANES) for side in range(2)]
        x_rows[:, :half] = sides[0][:, :half].astype(jnp.bfloat16)
        x_rows[:, half:] = sides[1][:, :half].astype(jnp.bfloat16)
        total += sides[0][:, half:] + sides[1][:, half:]
        where = pl.ds(pl.multiple_of(part * quarter, LANES), quarter)
        values = x_rows[...]
        for j in range(2):
            product = dot_nt(values, sgu[j, :, where])
            spairs[j] = product if number == 0 else spairs[j] + product

        def one_expert(e, carry):
            for j in range(2):
                product = dot_nt(values, gu[e, j, :, where])
                pairs[e, j] = product if number == 0 else pairs[e, j] + product
            return carry

        lax.fori_loop(0, local_experts, one_expert, 0, unroll=True)
    inverse = lax.rsqrt(total[:, :1] / width + norm_eps)
    routed = gate_all[...].reshape(all_rows, LANES)
    lanes = lax.broadcasted_iota(jnp.int32, (all_rows, LANES), 1)

    def activate(gate_part, up_part, weight):
        gate_part = gate_part * inverse
        up_part = up_part * inverse
        return (gate_part / (1.0 + jnp.exp(-gate_part)) * up_part * weight).astype(jnp.bfloat16)

    unit = first + lax.broadcasted_iota(jnp.int32, (all_rows, piece), 1)
    sact[...] = activate(spairs[0], spairs[1], jnp.where(unit >= ex * piece, 1.0, 0.0))

    def finish_expert(e, carry):
        weight = jnp.sum(
            jnp.where(lanes == ex * local_experts + e, routed, 0.0), axis=1, keepdims=True
        )
        act[e] = activate(pairs[e, 0], pairs[e, 1], weight)
        return carry

    lax.fori_loop(0, local_experts, finish_expert, 0)
    for copy in dn_copies:
        copy.wait()

    def down_part(part):
        where = pl.ds(pl.multiple_of(part * quarter, LANES), quarter)
        return lax.fori_loop(
            0,
            local_experts,
            lambda e, so_far: so_far + dot_nn(act[e], dn[e, :, where]),
            dot_nn(sact[...], sdn[:, where]),
            unroll=True,
        )

    p_copies = []
    for peer in hg_peers[::-1]:
        part_send[peer] = down_part(peer).astype(jnp.bfloat16)
        copy = pltpu.make_async_remote_copy(
            src_ref=part_send.at[peer],
            dst_ref=part_got.at[hg],
            send_sem=send_p.at[peer],
            recv_sem=recv_p.at[hg],
            device_id=(ex, peer),
            device_id_type=MESH,
        )
        copy.start()
        p_copies.append(copy)
    mine[...] = down_part(hg)
    for peer in hg_peers:
        arrived(part_got, peer, recv_p)
    summed = mine[...]
    for peer in hg_peers:
        summed += part_got[peer].astype(jnp.float32)
    row_part[...] = summed.reshape(n_ex, rows, quarter)
    r_copies = []
    for peer in ex_peers:
        copy = pltpu.make_async_remote_copy(
            src_ref=row_part.at[peer],
            dst_ref=row_got.at[ex],
            send_sem=send_r.at[peer],
            recv_sem=recv_r.at[ex],
            device_id=(peer, hg),
            device_id_type=MESH,
        )
        copy.start()
        r_copies.append(copy)
    final = hidden[...] + row_part[ex]
    for peer in ex_peers:
        arrived(row_got, peer, recv_r)
        final += row_got[peer]
    outs[1] = final
    for copy in gate_copies + attn_copies + x_copies + h_copies + p_copies + r_copies:
        copy.wait_send()


def local(
    residual_in,
    queries,
    new_latent,
    cache,
    lengths,
    value_up,
    out_proj,
    norm_gain,
    routes,
    gate_weights,
    expert_gate_up,
    expert_down,
    shared_gate_up,
    shared_down,
):
    n_ex, n_hg = lax.axis_size("ex"), lax.axis_size("hg")
    rows, slots, keyw = cache.shape
    heads, _, head_v = value_up.shape
    local_experts, _, units, width = expert_gate_up.shape
    quarter = width // n_hg
    piece = -(-(units // TILE) // n_ex) * TILE
    bf16, f32 = jnp.bfloat16, jnp.float32
    vmem, dma = pltpu.VMEM, pltpu.SemaphoreType.DMA
    in_vmem, in_hbm = pl.BlockSpec(memory_space=pltpu.VMEM), pl.BlockSpec(memory_space=pl.ANY)
    outs = pl.pallas_call(
        functools.partial(kernel, n_ex, n_hg),
        out_shape=jax.ShapeDtypeStruct((2, rows, quarter), f32),
        in_specs=[pl.BlockSpec(memory_space=pltpu.SMEM)] + [in_vmem] * 6 + [in_hbm] * 7,
        out_specs=in_vmem,
        scratch_shapes=[
            vmem((rows, keyw, slots), bf16),
            vmem(value_up.shape, bf16),
            vmem(out_proj.shape, bf16),
            vmem(expert_gate_up.shape, bf16),
            vmem(expert_down.shape, bf16),
            vmem((2, piece, width), bf16),
            vmem((piece, width), bf16),
            vmem((rows * heads, LATENT), f32),
            vmem((n_hg, rows, quarter), f32),
            vmem((n_hg, rows, quarter), f32),
            vmem((n_ex, rows, LANES), f32),
            vmem((n_hg, n_ex, 2 * rows, quarter // 2 + LANES), bf16),
            vmem((n_ex * rows, quarter), bf16),
            vmem((local_experts, 2, n_ex * rows, units), f32),
            vmem((2, n_ex * rows, piece), f32),
            vmem((local_experts, n_ex * rows, units), bf16),
            vmem((n_ex * rows, piece), bf16),
            vmem((n_ex * rows, quarter), f32),
            vmem((n_hg, n_ex * rows, quarter), bf16),
            vmem((n_hg, n_ex * rows, quarter), bf16),
            vmem((n_ex, rows, quarter), f32),
            vmem((n_ex, rows, quarter), f32),
            vmem((rows, quarter), f32),
            dma((rows,)),
            dma,
            dma,
            dma((local_experts,)),
            dma((local_experts,)),
            dma((2,)),
            dma((n_hg,)),
            dma((n_hg,)),
            dma((n_ex,)),
            dma((n_ex,)),
            dma((n_ex,)),
            dma((n_ex,)),
            dma((n_hg,)),
            dma((n_hg,)),
            dma((n_hg,)),
            dma((n_hg,)),
            dma((n_ex,)),
            dma((n_ex,)),
        ],
        compiler_params=pltpu.CompilerParams(
            collective_id=0, has_side_effects=True, vmem_limit_bytes=58 * 1024 * 1024
        ),
    )(
        lengths,
        residual_in,
        queries,
        new_latent,
        norm_gain.reshape(1, -1),
        routes,
        gate_weights,
        jnp.swapaxes(cache, 1, 2),
        value_up,
        out_proj,
        expert_gate_up,
        expert_down,
        shared_gate_up,
        shared_down,
    )
    return outs[0].astype(bf16), outs[1].astype(bf16)


def solution(mesh):
    placed = (
        P("ex", None),
        P("ex", "hg", None),
        P("ex", None),
        P("ex", None, None),
        P("ex"),
        P("hg", None, None),
        P("hg", None, None),
        P(),
        P("ex", None),
        P("ex", None),
        P("ex", None, "hg", None),
        P("ex", "hg", None),
        P(None, "hg", None),
        P("hg", None),
    )
    return jax.shard_map(
        local, mesh=mesh, in_specs=placed, out_specs=(P("ex", "hg"), P("ex", "hg")), check_vma=False
    )
```
